32 devices in a mesh: groups: 2 (over y), row: 8 (over z, x), col: 2 (over core).
Axes of the slice: x: 2, y: 2, z: 4, core: 2. Of those that a mesh axis runs over, the one named last changes fastest.
Arguments:
- tokens: bfloat16 [768, 8192], P(('groups', 'col'), 'row'), parts along dimension 0, may hold values from -6 to 6
- gate_up_blocks: bfloat16 [2, 2, 2048, 128, 128], P(None, 'col', 'row'), may hold values from -0.125 to 0.125
- gate_up_index: int32 [2, 2048], P('col', 'row'), may hold values from 0 to 511, as said below
- gate_up_count: int32 [2, 8], P('col', 'row'), may hold values from 1 to 256, as said below
- down_blocks: bfloat16 [2, 2048, 128, 128], P('col', 'row'), may hold values from -0.09375 to 0.09375
- down_index: int32 [2, 2048], P('col', 'row'), may hold values from 0 to 511, as said below
- down_count: int32 [2, 8], P('col', 'row'), may hold values from 1 to 256, as said below
- grad_out: bfloat16 [768, 8192], P(('groups', 'col'), 'row'), parts along dimension 0, may hold values from -6 to 6
Outputs:
- output: bfloat16 [768, 8192], P(('groups', 'col'), 'row'), parts along dimension 0
- grad_in: bfloat16 [768, 8192], P(('groups', 'col'), 'row'), parts along dimension 0
- grad_gate_up: float32 [2, 4, 2048, 128, 128], P(None, ('groups', 'col'), 'row'), parts along dimension 1
- grad_down: float32 [4, 2048, 128, 128], P(('groups', 'col'), 'row'), parts along dimension 0
The draws below stay inside these ranges and needn't reach their ends.
There are 2 independent parts, one for each index of `groups`. The reference program is written for one: setup_inputs(seed, part) draws one part's arguments, and reference() takes and returns one part's arrays. A program takes and returns all parts, laid end to end along the dimension named above; an argument that names none is the same for every part. Nothing has to cross between parts.
Inputs may be any that keep to these rules, and one draw needn't show every extreme that they name: `gate_up_index`: within each panel the 256 positions are distinct. `gate_up_count`: some panel has all 256 slots live. `down_index`: within each panel the 256 positions are distinct. `down_count`: some panel has all 256 slots live.
All inputs are finite; a program needn't handle non-finite values.
Results may differ from the reference program's by a relative error of at most 0.005.
Values may be sent and summed in bfloat16 or wider, within the bound.
A program may use at most 448 MiB of HBM per device.

```python
import jax
import jax.numpy as jnp
from jax import lax

D = 8192
FFW = 16384
BLK = 128
TOKENS = 384
HALF_ROWS = 32
PANEL_COLS = 16
SLOTS = 256
N_ROW = 8
N_COL = 2


def panel_positions(key, slot_count, panel_total):
    key_list = jax.random.split(key, N_COL * N_ROW)
    orders = jax.vmap(lambda one_key: jax.random.permutation(one_key, panel_total)[:slot_count])(key_list)
    return orders.reshape(N_COL, N_ROW * slot_count).astype(jnp.int32)


def block_counts(key, slot_count):
    first_key, second_key = jax.random.split(key)
    base_counts = jax.random.randint(first_key, (N_COL * N_ROW,), 1, slot_count + 1)
    chosen = jax.random.randint(second_key, (), 0, N_COL * N_ROW)
    base_counts = base_counts.at[chosen].set(slot_count)
    return base_counts.reshape(N_COL, N_ROW).astype(jnp.int32)


def draw_gate_up_index(key, part):
    key = jax.random.fold_in(key, 11)
    return panel_positions(key, SLOTS, HALF_ROWS * PANEL_COLS)


def draw_gate_up_count(key, part):
    key = jax.random.fold_in(key, 12)
    return block_counts(key, SLOTS)


def draw_down_index(key, part):
    key = jax.random.fold_in(key, 13)
    return panel_positions(key, SLOTS, HALF_ROWS * PANEL_COLS)


def draw_down_count(key, part):
    key = jax.random.fold_in(key, 14)
    return block_counts(key, SLOTS)


def levels(key, dims, cuts, smallest, high):
    gain = 1.0
    for axis_at, blocks in cuts:
        draws = jax.random.uniform(jax.random.fold_in(jax.random.fold_in(key, 6), axis_at), (blocks,), jnp.float32, smallest / len(cuts), high / len(cuts))
        gain = gain * jnp.repeat(jnp.exp(draws), dims[axis_at] // blocks).reshape((-1,) + (1,) * (len(dims) - 1 - axis_at))
    return gain


def centred(key, dims, deviation, most, pieces=(), held_as=jnp.bfloat16):
    array = jax.random.normal(key, dims, jnp.float32) * deviation
    if len(pieces) > 0:
        array = levels(key, dims, pieces, -0.22, 0.18) * array
    return jnp.clip(array, min=-most, max=most).astype(held_as)


def setup_inputs(seed: int = 0, part: int = 0) -> dict:
    arg_keys = jax.random.split(jax.random.key(seed), 9)
    part_keys = jax.random.split(jax.random.fold_in(arg_keys[8], part), 9)
    return {
        "tokens": centred(part_keys[0], (TOKENS, D), 1.0, 6.0, ((0, 2), (1, 8))),
        "gate_up_blocks": centred(arg_keys[1], (2, N_COL, N_ROW * SLOTS, BLK, BLK), (D // 4) ** -0.5, 0.125, ((1, 2), (2, 8))),
        "gate_up_index": draw_gate_up_index(jax.random.fold_in(arg_keys[8], 71), part),
        "gate_up_count": draw_gate_up_count(jax.random.fold_in(arg_keys[8], 71), part),
        "down_blocks": centred(arg_keys[4], (N_COL, N_ROW * SLOTS, BLK, BLK), (FFW // 4) ** -0.5, 0.09375, ((0, 2), (1, 8))),
        "down_index": draw_down_index(jax.random.fold_in(arg_keys[8], 71), part),
        "down_count": draw_down_count(jax.random.fold_in(arg_keys[8], 71), part),
        "grad_out": centred(part_keys[7], (TOKENS, D), 1.0, 6.0, ((0, 2), (1, 8))),
    }


def silu_parts(gate):
    sigmoid = jax.nn.sigmoid(gate)
    return gate * sigmoid, sigmoid * (1.0 + gate * (1.0 - sigmoid))


def one_hot(values, size, live):
    table = (values[:, None] == jnp.arange(size, dtype=jnp.int32)[None, :]).astype(jnp.float32)
    return table * live[:, None]


def reference(tokens, gate_up_blocks, gate_up_index, gate_up_count, down_blocks, down_index, down_count, grad_out):
    high = lax.Precision.HIGHEST
    half_rows = D // (N_COL * BLK)
    panel_cols = FFW // (N_ROW * BLK)
    d_blocks = D // BLK
    row_total = tokens.shape[0]
    slot_range = jnp.arange(SLOTS, dtype=jnp.int32)
    halves = jnp.arange(N_COL, dtype=jnp.int32)[:, None]
    tok_blocks = tokens.reshape(row_total, d_blocks, BLK)
    grad_blocks = grad_out.reshape(row_total, d_blocks, BLK)
    weights_gu = gate_up_blocks.reshape(2, N_COL, N_ROW, SLOTS, BLK, BLK).transpose(2, 0, 1, 3, 4, 5)
    index_gu = gate_up_index.reshape(N_COL, N_ROW, SLOTS).transpose(1, 0, 2)
    count_gu = gate_up_count.T
    weights_dn = down_blocks.reshape(N_COL, N_ROW, SLOTS, BLK, BLK).transpose(1, 0, 2, 3, 4)
    index_dn = down_index.reshape(N_COL, N_ROW, SLOTS).transpose(1, 0, 2)
    count_dn = down_count.T

    def panel_step(state_pair, inputs):
        out_sum, in_sum = state_pair
        w_gu, i_gu, c_gu, w_dn, i_dn, c_dn = inputs
        live_gu = (slot_range[None, :] < c_gu[:, None]).reshape(-1).astype(jnp.float32)
        live_dn = (slot_range[None, :] < c_dn[:, None]).reshape(-1).astype(jnp.float32)
        d_of_gu = (halves * half_rows + i_gu // panel_cols).reshape(-1).astype(jnp.int32)
        f_of_gu = (i_gu % panel_cols).reshape(-1).astype(jnp.int32)
        f_of_dn = (i_dn // half_rows).reshape(-1).astype(jnp.int32)
        d_of_dn = (halves * half_rows + i_dn % half_rows).reshape(-1).astype(jnp.int32)
        ff_gu = one_hot(f_of_gu, panel_cols, live_gu)
        dd_gu = one_hot(d_of_gu, d_blocks, live_gu)
        ff_dn = one_hot(f_of_dn, panel_cols, live_dn)
        dd_dn = one_hot(d_of_dn, d_blocks, live_dn)
        wgu = w_gu.reshape(2, N_COL * SLOTS, BLK, BLK).astype(jnp.float32)
        wdn = w_dn.reshape(N_COL * SLOTS, BLK, BLK).astype(jnp.float32)
        x_sel = tok_blocks[:, d_of_gu].astype(jnp.float32)
        term_blocks = jnp.einsum('tsk,gskn->gstn', x_sel, wgu, precision=high)
        gate_up = jnp.einsum('gstn,sf->gtfn', term_blocks, ff_gu, precision=high).reshape(2, row_total, panel_cols * BLK)
        act_f, slope_term = silu_parts(gate_up[0])
        hidden = (act_f * gate_up[1]).astype(jnp.bfloat16)
        h_sel = hidden.reshape(row_total, panel_cols, BLK)[:, f_of_dn].astype(jnp.float32)
        out_terms = jnp.einsum('tsk,skn->stn', h_sel, wdn, precision=high)
        out_part = jnp.einsum('stn,sd->tdn', out_terms, dd_dn, precision=high)
        g_sel = grad_blocks[:, d_of_dn].astype(jnp.float32)
        back_terms = jnp.einsum('tsn,skn->stk', g_sel, wdn, precision=high)
        grad_hidden = jnp.einsum('stk,sf->tfk', back_terms, ff_dn, precision=high).reshape(row_total, panel_cols * BLK)
        grad_gate = (grad_hidden * gate_up[1] * slope_term).astype(jnp.bfloat16)
        grad_up = (grad_hidden * act_f).astype(jnp.bfloat16)
        grad_pair = jnp.stack([grad_gate, grad_up]).reshape(2, row_total, panel_cols, BLK)
        gu_sel = grad_pair[:, :, f_of_gu].astype(jnp.float32)
        in_terms = jnp.einsum('gtsn,gskn->stk', gu_sel, wgu, precision=high)
        in_part = jnp.einsum('stk,sd->tdk', in_terms, dd_gu, precision=high)
        dw_gu = jnp.einsum('tsk,gtsn->gskn', x_sel, gu_sel, precision=high) * live_gu[None, :, None, None]
        dw_dn = jnp.einsum('tsk,tsn->skn', h_sel, g_sel, precision=high) * live_dn[:, None, None]
        return (out_sum + out_part, in_sum + in_part), (dw_gu.reshape(2, N_COL, SLOTS, BLK, BLK), dw_dn.reshape(N_COL, SLOTS, BLK, BLK))

    zero_sum = jnp.zeros((row_total, d_blocks, BLK), jnp.float32)
    (out_sum, in_sum), (dw_gu, dw_dn) = lax.scan(panel_step, (zero_sum, zero_sum), (weights_gu, index_gu, count_gu, weights_dn, index_dn, count_dn))
    grad_gate_up = dw_gu.transpose(1, 2, 0, 3, 4, 5).reshape(2, N_COL, N_ROW * SLOTS, BLK, BLK)
    grad_down = dw_dn.transpose(1, 0, 2, 3, 4).reshape(N_COL, N_ROW * SLOTS, BLK, BLK)
    output = out_sum.reshape(row_total, D).astype(jnp.bfloat16)
    grad_in = in_sum.reshape(row_total, D).astype(jnp.bfloat16)
    return (output, grad_in, grad_gate_up, grad_down)
```

```python
import functools

import jax
import jax.numpy as jnp
from jax import lax
from jax.experimental import pallas as pl
from jax.experimental.pallas import tpu as pltpu
from jax.sharding import PartitionSpec as P

FFW = 16384
F32 = jnp.float32
BF16 = jnp.bfloat16


def clear(ref):
    def body(i, carry):
        ref[i] = jnp.zeros(ref.shape[1:], ref.dtype)
        return carry

    lax.fori_loop(0, ref.shape[0], body, 0)


def live_slots(count, chunk):
    base = pl.program_id(0) * chunk
    return base, jnp.clip(count[0] - base, 0, chunk)


def dot_nt(a, b):
    return lax.dot_general(a, b, (((1,), (1,)), ((), ())), preferred_element_type=F32)


def gate_up_kernel(cols, chunk, index, count, x, w, acc):
    @pl.when(pl.program_id(0) == 0)
    def _():
        clear(acc)

    base, live = live_slots(count, chunk)

    def body(i, carry):
        p = index[base + i]
        pair = jnp.concatenate([w[0, i], w[1, i]], axis=1)
        acc[lax.rem(p, cols)] += jnp.dot(x[lax.div(p, cols)], pair, preferred_element_type=F32)
        return carry

    lax.fori_loop(0, live, body, 0)


def down_kernel(rows, chunk, index, count, h, g, w, out, back):
    @pl.when(pl.program_id(0) == 0)
    def _():
        clear(out)
        clear(back)

    base, live = live_slots(count, chunk)

    def body(i, carry):
        p = index[base + i]
        f, d = lax.div(p, rows), lax.rem(p, rows)
        out[d] += jnp.dot(h[f], w[i], preferred_element_type=F32)
        back[f] += dot_nt(g[d], w[i])
        return carry

    lax.fori_loop(0, live, body, 0)


def grad_in_kernel(cols, chunk, index, count, grads, w, out):
    @pl.when(pl.program_id(0) == 0)
    def _():
        clear(out)

    base, live = live_slots(count, chunk)

    def body(i, carry):
        p = index[base + i]
        pair = jnp.concatenate([w[0, i], w[1, i]], axis=1)
        out[lax.div(p, cols)] += dot_nt(grads[lax.rem(p, cols)], pair)
        return carry

    lax.fori_loop(0, live, body, 0)


def grad_gate_up_kernel(cols, chunk, index, count, xt, grads, dw):
    base, live = live_slots(count, chunk)
    size = dw.shape[-1]

    def body(i, carry):
        p = index[base + i]
        both = jnp.dot(xt[lax.div(p, cols)], grads[lax.rem(p, cols)], preferred_element_type=F32)
        dw[0, i] = both[:, :size]
        dw[1, i] = both[:, size:]
        return carry

    def empty(i, carry):
        dw[0, i] = jnp.zeros((size, size), F32)
        dw[1, i] = jnp.zeros((size, size), F32)
        return carry

    lax.fori_loop(0, live, body, 0)
    lax.fori_loop(live, chunk, empty, 0)


def grad_down_kernel(rows, chunk, index, count, ht, g, dw):
    base, live = live_slots(count, chunk)
    size = dw.shape[-1]

    def body(i, carry):
        p = index[base + i]
        dw[i] = jnp.dot(ht[lax.div(p, rows)], g[lax.rem(p, rows)], preferred_element_type=F32)
        return carry

    def empty(i, carry):
        dw[i] = jnp.zeros((size, size), F32)
        return carry

    lax.fori_loop(0, live, body, 0)
    lax.fori_loop(live, chunk, empty, 0)


def whole(shape):
    return pl.BlockSpec(shape, lambda *_: (0,) * len(shape))


def pair_chunk(chunk, size):
    return pl.BlockSpec((2, chunk, size, size), lambda s, *_: (0, s, 0, 0))


def one_chunk(chunk, size):
    return pl.BlockSpec((chunk, size, size), lambda s, *_: (s, 0, 0))


def run(kernel, steps, flops, index, count, operands, in_specs, out_shape, out_specs):
    return pl.pallas_call(
        kernel,
        out_shape=out_shape,
        grid_spec=pltpu.PrefetchScalarGridSpec(
            num_scalar_prefetch=2,
            grid=(steps,),
            in_specs=in_specs,
            out_specs=out_specs,
        ),
        compiler_params=pltpu.CompilerParams(
            dimension_semantics=("arbitrary",), vmem_limit_bytes=50 * 1024 * 1024
        ),
        cost_estimate=pl.CostEstimate(flops=flops, bytes_accessed=32 << 20, transcendentals=0),
    )(index, count, *operands)


def per_device(
    tokens,
    gate_up_blocks,
    gate_up_index,
    gate_up_count,
    down_blocks,
    down_index,
    down_count,
    grad_out,
):
    n_row = lax.axis_size("row")
    n_col = lax.axis_size("col")
    col = lax.axis_index("col")
    size = gate_up_blocks.shape[-1]
    slots = gate_up_blocks.shape[2]
    width = tokens.shape[1] * n_row
    half = width // n_col
    rows = half // size
    cols = FFW // (n_row * size)
    t = tokens.shape[0]
    both = 2 * t
    chunk = min(32, slots)
    steps = slots // chunk
    unit = 4 * slots * both * size * size
    swap = [(0, 1), (1, 0)]

    def exchange(a):
        return lax.ppermute(a, "col", swap)

    def spread(a):
        all_width = lax.all_gather(a, "row", axis=1, tiled=True)
        own = lax.dynamic_slice_in_dim(all_width, col * half, half, 1)
        other = exchange(lax.dynamic_slice_in_dim(all_width, (1 - col) * half, half, 1))
        return jnp.concatenate([own, other], axis=0).reshape(both, rows, size)

    x_flat = spread(tokens)
    g_flat = spread(grad_out)
    x = x_flat.transpose(1, 0, 2)
    xt = x_flat.transpose(1, 2, 0)
    g = g_flat.transpose(1, 0, 2)
    w_gu = gate_up_blocks[:, 0]
    w_dn = down_blocks[0]
    gu_index, gu_count = gate_up_index[0], gate_up_count[0]
    dn_index, dn_count = down_index[0], down_count[0]

    def shape(*dims):
        return jax.ShapeDtypeStruct(dims, F32)

    part = run(
        functools.partial(gate_up_kernel, cols, chunk), steps, unit, gu_index, gu_count, (x, w_gu),
        [whole((rows, both, size)), pair_chunk(chunk, size)],
        shape(cols, both, 2 * size), whole((cols, both, 2 * size)),
    )
    gate_up = part[:, :t] + exchange(part[:, t:])
    gate, up = gate_up[..., :size], gate_up[..., size:]
    sigmoid = jax.nn.sigmoid(gate)
    act = gate * sigmoid
    slope = sigmoid * (1.0 + gate * (1.0 - sigmoid))
    hidden = (act * up).astype(BF16)
    h = jnp.concatenate([hidden, exchange(hidden)], axis=1)
    out_part, back_part = run(
        functools.partial(down_kernel, rows, chunk), steps, unit, dn_index, dn_count, (h, g, w_dn),
        [whole((cols, both, size)), whole((rows, both, size)), one_chunk(chunk, size)],
        (shape(rows, both, size), shape(cols, both, size)),
        (whole((rows, both, size)), whole((cols, both, size))),
    )

    def collect(a):
        own, other = a[:, :t], exchange(a[:, t:])
        full = jnp.where(
            col == 0,
            jnp.concatenate([own, other], axis=0),
            jnp.concatenate([other, own], axis=0),
        )
        mine = lax.psum_scatter(full, "row", scatter_dimension=0, tiled=True)
        return mine.transpose(1, 0, 2).reshape(t, width // n_row).astype(BF16)

    output = collect(out_part)
    grad_hidden = back_part[:, :t] + exchange(back_part[:, t:])
    grads_own = jnp.concatenate(
        [(grad_hidden * up * slope).astype(BF16), (grad_hidden * act).astype(BF16)], axis=-1
    )
    grads = jnp.concatenate([grads_own, exchange(grads_own)], axis=1)
    in_part = run(
        functools.partial(grad_in_kernel, cols, chunk), steps, unit, gu_index, gu_count, (grads, w_gu),
        [whole((cols, both, 2 * size)), pair_chunk(chunk, size)],
        shape(rows, both, size), whole((rows, both, size)),
    )
    grad_in = collect(in_part)
    dw_gu = run(
        functools.partial(grad_gate_up_kernel, cols, chunk), steps, unit, gu_index, gu_count, (xt, grads),
        [whole((rows, size, both)), whole((cols, both, 2 * size))],
        shape(2, slots, size, size), pair_chunk(chunk, size),
    )
    dw_dn = run(
        functools.partial(grad_down_kernel, rows, chunk), steps, unit // 2, dn_index, dn_count,
        (h.transpose(0, 2, 1), g),
        [whole((cols, size, both)), whole((rows, both, size))],
        shape(slots, size, size), one_chunk(chunk, size),
    )
    return (output, grad_in, dw_gu[:, None], dw_dn[None])


def solution(mesh):
    placed = (
        P(("groups", "col"), "row"),
        P(None, "col", "row", None, None),
        P("col", "row"),
        P("col", "row"),
        P("col", "row", None, None),
        P("col", "row"),
        P("col", "row"),
        P(("groups", "col"), "row"),
    )
    return jax.shard_map(
        per_device,
        mesh=mesh,
        in_specs=placed,
        out_specs=(
            P(("groups", "col"), "row"),
            P(("groups", "col"), "row"),
            P(None, ("groups", "col"), "row", None, None),
            P(("groups", "col"), "row", None, None),
        ),
        check_vma=False,
    )
```
